32 devices in a mesh: row: 8 (over y, x, core), col: 4 (over z).
Axes of the slice: x: 2, y: 2, z: 4, core: 2. Of those that a mesh axis runs over, the one named last changes fastest.
Arguments:
- spectra: bfloat16 [32, 4096, 512], P(None, ('row', 'col')), may hold values from -6 to 6
- quality: int32 [4096], P(('row', 'col')), may hold values 0 or 1
- tile_mask: int32 [32, 32], replicated, may hold values 0 or 1
Outputs:
- correlations: bfloat16 [64, 4096, 4096], P(None, 'row', 'col')
The draws below stay inside these ranges and needn't reach their ends.
All inputs are finite; a program needn't handle non-finite values. No bound on the sum of `quality` on one device may be relied on, other than what follows from the above.
Results may differ from the reference program's by a relative error of at most 0.0066.
Values may be sent and summed in bfloat16 or wider, within the bound.
No kernel may reach another device: no remote copies, remote signals or barrier semaphores. Data moves between devices by JAX's collectives and lax.ppermute only.
A program may use at most 256 MiB of HBM per device.

```python
import math
import jax
import jax.numpy as jnp
from jax import lax

C = 4096
F = 32
LAGS = 64
W = 256
BLK = 128


def with_ends(drawn, stream_key, smallest, largest):
    extent = drawn.shape
    place = [jax.random.randint(jax.random.fold_in(stream_key, axis), (), 0, extent[axis]) for axis in range(len(extent))]
    drawn = drawn.at[tuple(place)].set(smallest)
    longest = extent.index(max(extent))
    place[longest] = (place[longest] + 1) % extent[longest]
    return drawn.at[tuple(place)].set(largest)


def block_levels(rng, shape, shards, low, top_value):
    loudness = 1.0
    for dim, parts in shards:
        draws = jax.random.uniform(jax.random.fold_in(jax.random.fold_in(rng, 6), dim), (parts,), jnp.float32, low / len(shards), top_value / len(shards))
        loudness = loudness * jnp.repeat(jnp.exp(draws), shape[dim] // parts).reshape((-1,) + (1,) * (len(shape) - 1 - dim))
    return loudness


def noise(stream_key, extent, width, reach, pieces=(), kind=jnp.bfloat16):
    drawn = width * jax.random.normal(stream_key, extent, jnp.float32)
    if pieces:
        drawn = drawn * block_levels(stream_key, extent, pieces, -0.22, 0.18)
    return jnp.clip(drawn, -reach, reach).astype(kind)


def setup_inputs(seed: int = 0) -> dict:
    streams_of = jax.random.split(jax.random.key(seed), 4)
    spectra = noise(streams_of[0], (F, C, 2 * W), 1.0, 6.0, ((1, 32),))
    quality = with_ends((jax.random.randint(streams_of[1], (C,), 0, 8) < 7).astype(jnp.int32), jax.random.fold_in(streams_of[1], 1), 0, 1)
    tile_mask = with_ends((jax.random.randint(streams_of[2], (C // BLK, C // BLK), 0, 4) < 3).astype(jnp.int32), jax.random.fold_in(streams_of[2], 1), 0, 1)
    return dict(spectra=spectra, quality=quality, tile_mask=tile_mask)


def whiten(spectra, quality):
    values = spectra.astype(jnp.float32)
    half_width = values.shape[2] // 2
    real_part = values[:, :, :half_width]
    imag_part = values[:, :, half_width:]
    energy = real_part * real_part + imag_part * imag_part
    mean_energy = lax.optimization_barrier(jnp.mean(energy, axis=0, keepdims=True))
    factor = quality.astype(jnp.float32)[None, :, None] / jnp.sqrt(energy + mean_energy + 1e-06)
    return jnp.concatenate([real_part * factor, imag_part * factor], axis=2).astype(jnp.bfloat16)

def make_basis():
    lag_offset = jnp.arange(LAGS, dtype=jnp.float32) - LAGS / 2
    frequency = jnp.arange(F, dtype=jnp.float32) + 1.0
    angles = 2.0 * math.pi * frequency[None, :] * lag_offset[:, None] / (2.0 * LAGS)
    return jnp.stack([jnp.cos(angles), -jnp.sin(angles)], axis=1).astype(jnp.bfloat16)

def reference(spectra, quality, tile_mask):
    white = whiten(spectra, quality)
    half_width = white.shape[2] // 2
    turned = jnp.concatenate([-white[:, :, half_width:], white[:, :, :half_width]], axis=2)
    both_parts = jnp.concatenate([white, turned], axis=1).astype(jnp.float32)
    lag_basis = make_basis().astype(jnp.float32)
    norm_scale = 1.0 / math.sqrt(W * F)
    col_tiles = C // BLK

    def one_block(block_index):
        rows_here = lax.dynamic_slice_in_dim(white, block_index * BLK, BLK, 1).astype(jnp.float32)
        cross_spec = jnp.einsum('fiw,fjw->fij', rows_here, both_parts).astype(jnp.bfloat16)
        cross_spec = cross_spec.astype(jnp.float32).reshape(F, BLK, 2, C)
        lagged = jnp.einsum('lpf,fipj->lij', lag_basis, cross_spec)
        mask_tiles = lax.dynamic_index_in_dim(tile_mask, block_index, 0, keepdims=False).astype(jnp.float32)
        mask_row = jnp.broadcast_to(mask_tiles[:, None], (col_tiles, BLK)).reshape(C)
        return (lagged * norm_scale * mask_row[None, None, :]).astype(jnp.bfloat16)
    blocks = lax.map(one_block, jnp.arange(C // BLK).astype(jnp.int32))
    return jnp.transpose(blocks, (1, 0, 2, 3)).reshape(LAGS, C, C)
```

```python
import functools
import math

import jax
import jax.numpy as jnp
import numpy as np
from jax import lax
from jax.experimental import pallas as pl
from jax.experimental.pallas import tpu as pltpu
from jax.sharding import PartitionSpec as P

BLK = 128
LAGS = 64
PARTS = 4
GROUP = 8
VMEM_BYTES = 48 * 1024 * 1024
AXES = ("row", "col")


def whiten(spectra, quality):
    values = spectra.astype(jnp.float32)
    half_width = values.shape[2] // 2
    real_part = values[:, :, :half_width]
    imag_part = values[:, :, half_width:]
    energy = real_part * real_part + imag_part * imag_part
    mean_energy = jnp.mean(energy, axis=0, keepdims=True)
    factor = quality.astype(jnp.float32)[None, :, None] / jnp.sqrt(energy + mean_energy + 1e-06)
    return jnp.concatenate([real_part * factor, imag_part * factor], axis=2).astype(jnp.bfloat16)


def lag_angles(bins):
    lag_offset = np.arange(LAGS, dtype=np.float32) - np.float32(LAGS / 2)
    frequency = np.arange(bins, dtype=np.float32) + np.float32(1.0)
    scaled = np.float32(2.0 * math.pi) * frequency[None, :]
    return (scaled * lag_offset[:, None]) / np.float32(2.0 * LAGS)


def general_plan(mesh, spectra, quality, tile_mask):
    bins, _, width = spectra.shape
    row_size, col_size = mesh.shape["row"], mesh.shape["col"]
    white = whiten(spectra, quality)
    row_block = lax.all_gather(white, "col", axis=1, tiled=True)
    row_index, col_index = lax.axis_index("row"), lax.axis_index("col")
    row_count = row_block.shape[1]
    col_count = row_count * row_size // col_size
    share_of = row_size // col_size
    zeros = jnp.zeros_like(row_block)
    sectioned = jnp.concatenate(
        [jnp.where(row_index == share_of * col_index + s, row_block, zeros) for s in range(share_of)], axis=1
    )
    share = lax.psum_scatter(sectioned, "row", scatter_dimension=1, tiled=True)
    col_block = lax.all_gather(share, "row", axis=1, tiled=True)
    half_width = width // 2
    turned = jnp.concatenate([-col_block[:, :, half_width:], col_block[:, :, :half_width]], axis=2)
    both_parts = jnp.concatenate([col_block, turned], axis=1)
    angles = lag_angles(bins)
    basis = jnp.asarray(np.stack([np.cos(angles), -np.sin(angles)], axis=1)).astype(jnp.bfloat16)
    mask = jnp.repeat(jnp.repeat(tile_mask.astype(jnp.float32), BLK, axis=0), BLK, axis=1)
    local_mask = lax.dynamic_slice(mask, (row_index * row_count, col_index * col_count), (row_count, col_count))
    norm_scale = 1.0 / math.sqrt(half_width * bins)
    step = math.gcd(row_count, BLK)

    def fill(index, result):
        rows_here = lax.dynamic_slice_in_dim(row_block, index * step, step, 1)
        cross = jnp.einsum("fiw,fjw->fij", rows_here, both_parts, preferred_element_type=jnp.float32)
        cross = cross.astype(jnp.bfloat16).reshape(bins, step, 2, col_count)
        lagged = jnp.einsum("lpf,fipj->lij", basis, cross, preferred_element_type=jnp.float32)
        mask_rows = lax.dynamic_slice_in_dim(local_mask, index * step, step, 0)
        piece = (lagged * norm_scale * mask_rows[None]).astype(jnp.bfloat16)
        return lax.dynamic_update_slice_in_dim(result, piece, index * step, 1)

    initial = jnp.zeros((LAGS, row_count, col_count), jnp.bfloat16)
    return lax.fori_loop(0, row_count // step, fill, initial)


def whiten_kernel(spectra_ref, quality_ref, *out_refs):
    bins, _, width = spectra_ref.shape
    half_width = width // 2
    per = bins // len(out_refs)
    total = jnp.zeros((spectra_ref.shape[1], half_width), jnp.float32)
    for f in range(bins):
        real_part = spectra_ref[f, :, :half_width].astype(jnp.float32)
        imag_part = spectra_ref[f, :, half_width:].astype(jnp.float32)
        total = total + (real_part * real_part + imag_part * imag_part)
    offset = total * (1.0 / bins) + 1e-06
    quality = quality_ref[...].astype(jnp.float32)
    for f in range(bins):
        real_part = spectra_ref[f, :, :half_width].astype(jnp.float32)
        imag_part = spectra_ref[f, :, half_width:].astype(jnp.float32)
        factor = quality * lax.rsqrt(real_part * real_part + imag_part * imag_part + offset)
        out_refs[f // per][f % per, :, :half_width] = (real_part * factor).astype(jnp.bfloat16)
        out_refs[f // per][f % per, :, half_width:] = (imag_part * factor).astype(jnp.bfloat16)


def whiten_parts(spectra, quality):
    bins, channels, width = spectra.shape
    per = bins // PARTS
    rows = 16
    return pl.pallas_call(
        whiten_kernel,
        grid=(channels // rows,),
        in_specs=[
            pl.BlockSpec((bins, rows, width), lambda i: (0, i, 0)),
            pl.BlockSpec((rows, 1), lambda i: (i, 0)),
        ],
        out_specs=[pl.BlockSpec((per, rows, width), lambda i: (0, i, 0))] * PARTS,
        out_shape=[jax.ShapeDtypeStruct((per, channels, width), jnp.bfloat16)] * PARTS,
        compiler_params=pltpu.CompilerParams(vmem_limit_bytes=VMEM_BYTES),
        name="whiten",
    )(spectra, quality[:, None])


def pick_kernel(choice_ref, *refs):
    sources, target_ref, sem = refs[:-2], refs[-2], refs[-1]
    block = target_ref.shape[0]
    first = pl.program_id(0) * block
    for index, source in enumerate(sources):

        @pl.when(choice_ref[0] == index)
        def _():
            pltpu.make_async_copy(source.at[pl.ds(first, block)], target_ref, sem).start()

    pltpu.make_async_copy(sources[0].at[pl.ds(first, block)], target_ref, sem).wait()


def pick(choice, sources):
    shape = sources[0]
    moved = 2 * math.prod(shape.shape) * 2
    block = shape.shape[0] // 2
    return pl.pallas_call(
        pick_kernel,
        grid_spec=pltpu.PrefetchScalarGridSpec(
            num_scalar_prefetch=1,
            grid=(shape.shape[0] // block,),
            in_specs=[pl.BlockSpec(memory_space=pl.ANY)] * len(sources),
            out_specs=pl.BlockSpec((block,) + shape.shape[1:], lambda i, _: (i, 0, 0)),
            scratch_shapes=[pltpu.SemaphoreType.DMA],
        ),
        out_shape=jax.ShapeDtypeStruct(shape.shape, shape.dtype),
        cost_estimate=pl.CostEstimate(flops=0, bytes_accessed=moved, transcendentals=0),
        name="pick",
    )(choice, *sources)


def correlate_kernel(units, parts, offset_ref, scale_ref, *refs):
    n_sets = 1 + max(max(u) for u in units)
    x_refs = [refs[s * parts : (s + 1) * parts] for s in range(n_sets)]
    rest = refs[n_sets * parts :]
    y_refs = [[rest[(2 * s + h) * parts : (2 * s + h + 1) * parts] for h in range(2)] for s in range(n_sets)]
    rest = rest[2 * n_sets * parts :]
    even_ref, odd_ref = rest[:2]
    out_ref, x_buf, y_buf, cross, out_buf, in_sem, out_sem = rest[-7:]
    per, rows, width = x_buf.shape[1:]
    half_width = width // 2
    groups = rows // GROUP
    cols = 2 * rows
    lags = out_buf.shape[1]
    half = lags // 2
    steps = len(units) * parts

    def copies_in(a, b, c, slot):
        return [
            pltpu.make_async_copy(x_refs[a][c], x_buf.at[slot], in_sem.at[slot, 0]),
            pltpu.make_async_copy(y_refs[b][0][c], y_buf.at[slot, :, pl.ds(0, rows)], in_sem.at[slot, 1]),
            pltpu.make_async_copy(y_refs[b][1][c], y_buf.at[slot, :, pl.ds(rows, rows)], in_sem.at[slot, 2]),
        ]

    def fetch(step):
        slot = lax.rem(step, 2)
        for s in range(steps):
            a, b = units[s // parts]

            @pl.when(step == s)
            def _():
                for copy in copies_in(a, b, s % parts, slot):
                    copy.start()

    def copies_out(unit, slot):
        row = pl.multiple_of(offset_ref[0, unit], rows)
        return [
            pltpu.make_async_copy(
                out_buf.at[slot, :, :, pl.ds(h * rows, rows)],
                out_ref.at[:, pl.ds(row, rows), pl.ds(pl.multiple_of(offset_ref[1 + h, unit], rows), rows)],
                out_sem.at[slot, h],
            )
            for h in range(2)
        ]

    fetch(0)

    @pl.loop(0, steps)
    def _(step):
        slot = lax.rem(step, 2)
        unit = step // parts
        part = lax.rem(step, parts)

        @pl.when(step + 1 < steps)
        def _():
            fetch(step + 1)

        for copy in copies_in(units[0][0], units[0][1], 0, slot):
            copy.wait()

        @pl.loop(0, per // 2)
        def _(pair):
            results = []
            for f in range(2):
                x = x_buf[slot, 2 * pair + f]
                y = y_buf[slot, 2 * pair + f]
                turned = jnp.concatenate([x[:, half_width:], -x[:, :half_width]], axis=1)
                stacked = jnp.concatenate([x, turned], axis=0)
                product = lax.dot_general(stacked, y, (((1,), (1,)), ((), ())), preferred_element_type=jnp.float32)
                results.append(product.reshape(2 * groups, GROUP, cols))
            both = jnp.concatenate(results, axis=1).astype(jnp.bfloat16)
            place = pl.multiple_of((part * (per // 2) + pair) * 2 * GROUP, 2 * GROUP)
            cross[:, pl.ds(place, 2 * GROUP), :] = both

        @pl.when(part == parts - 1)
        def _():
            out_slot = lax.rem(unit, 2)

            @pl.when(unit >= 2)
            def _():
                for copy in copies_out(unit - 2, out_slot):
                    copy.wait()

            scale = jnp.concatenate(
                [jnp.full((1, 1, rows), scale_ref[h, unit], jnp.float32) for h in range(2)], axis=2
            )

            @pl.loop(0, groups // 2)
            def _(two):
                evens, odds = [], []
                for g in range(2):
                    even = jnp.dot(even_ref[...], cross[2 * two + g], preferred_element_type=jnp.float32)
                    odd = jnp.dot(odd_ref[...], cross[groups + 2 * two + g], preferred_element_type=jnp.float32)
                    evens.append(even.reshape(half + 1, GROUP, cols))
                    odds.append(odd.reshape(half, GROUP, cols))
                even = jnp.concatenate(evens, axis=1) * scale
                odd = jnp.concatenate(odds, axis=1) * scale
                here = pl.ds(pl.multiple_of(two * 2 * GROUP, 2 * GROUP), 2 * GROUP)
                out_buf[out_slot, half, here, :] = even[0].astype(jnp.bfloat16)
                out_buf[out_slot, 0, here, :] = (even[half] + odd[0]).astype(jnp.bfloat16)
                for d in range(1, half):
                    out_buf[out_slot, half + d, here, :] = (even[d] - odd[d]).astype(jnp.bfloat16)
                    out_buf[out_slot, half - d, here, :] = (even[d] + odd[d]).astype(jnp.bfloat16)

            for copy in copies_out(unit, out_slot):
                copy.start()

    for unit in range(max(0, len(units) - 2), len(units)):
        for copy in copies_out(unit, unit % 2):
            copy.wait()


def lag_matrices(bins):
    half = LAGS // 2
    angles = lag_angles(bins)[half:]
    last = -lag_angles(bins)[0]
    cosine = np.concatenate([np.cos(angles), np.cos(last)[None]], axis=0)
    sine = np.concatenate([np.sin(last)[None], np.sin(angles)[1:]], axis=0)

    def spread(table):
        table = table.astype(jnp.bfloat16).astype(np.float32)
        return jnp.asarray(np.kron(table, np.eye(GROUP, dtype=np.float32)).astype(jnp.bfloat16))

    return spread(cosine), spread(sine)


def correlate(units, offsets, scales, rows_sets, cols_sets, matrices, out, out_shape):
    parts = len(rows_sets[0])
    per, rows, width = rows_sets[0][0].shape
    bins = per * parts
    n_sets = 1 + max(max(u) for u in units)
    operands = []
    for s in range(n_sets):
        operands += rows_sets[s]
    for s in range(n_sets):
        for h in range(2):
            operands += cols_sets[s][h]
    any_spec = pl.BlockSpec(memory_space=pl.ANY)
    vmem_spec = pl.BlockSpec(memory_space=pltpu.VMEM)
    n_ops = len(operands)
    before = [] if out is None else [out]
    pairs = len(units) * rows * 2 * rows
    flops = pairs * (bins * width * 4 + 2 * LAGS * bins * GROUP)
    moved = len(units) * (3 * bins * rows * width * 2 + LAGS * 2 * rows * rows * 2)
    return pl.pallas_call(
        functools.partial(correlate_kernel, units, parts),
        grid_spec=pltpu.PrefetchScalarGridSpec(
            num_scalar_prefetch=2,
            grid=(1,),
            in_specs=[any_spec] * n_ops + [vmem_spec] * 2 + [any_spec] * len(before),
            out_specs=any_spec,
            scratch_shapes=[
                pltpu.VMEM((2, per, rows, width), jnp.bfloat16),
                pltpu.VMEM((2, per, 2 * rows, width), jnp.bfloat16),
                pltpu.VMEM((2 * rows // GROUP, bins * GROUP, 2 * rows), jnp.bfloat16),
                pltpu.VMEM((2, LAGS, rows, 2 * rows), jnp.bfloat16),
                pltpu.SemaphoreType.DMA((2, 3)),
                pltpu.SemaphoreType.DMA((2, 2)),
            ],
        ),
        out_shape=jax.ShapeDtypeStruct(out_shape, jnp.bfloat16),
        input_output_aliases={2 + n_ops + 2: 0} if before else {},
        cost_estimate=pl.CostEstimate(flops=flops, bytes_accessed=moved, transcendentals=0),
        compiler_params=pltpu.CompilerParams(vmem_limit_bytes=VMEM_BYTES),
        name="correlate",
    )(offsets, scales, *operands, *matrices, *before)


def line_sets(size):
    table = []
    for j in range(1, size):
        entry = []
        for z in range(size):
            if 2 * z < size:
                entry.append(("dn", j - 1) if z + j < size else ("up", j - size + z))
            else:
                entry.append(("up", j - 1) if z - j >= 0 else ("dn", j - 1 - z))
        table.append(entry)
    return table


def owner(z, arrival):
    way, hops = arrival
    return z + 1 + hops if way == "dn" else z - 1 - hops


def line_plan(mesh, spectra, quality, tile_mask):
    row_size, col_size = mesh.shape["row"], mesh.shape["col"]
    chips = row_size // 2
    bins, channels, _ = spectra.shape
    tiles = channels // BLK
    assert tiles == 1
    row_index, col_index = lax.axis_index("row"), lax.axis_index("col")
    core = row_index % 2
    ring = [i ^ (i >> 1) for i in range(chips)]
    place = [ring.index(k) for k in range(chips)]

    def send(values, moves):
        pairs = [(r * col_size + c, s * col_size + d) for (r, c), (s, d) in moves]
        return lax.ppermute(values, AXES, pairs)

    every = [(r, c) for r in range(row_size) for c in range(col_size)]

    def send_up(values, hop):
        return send(values, [((r, c), (r, c + 1)) for r, c in every if hop <= c < col_size - 1])

    def send_down(values, hop):
        return send(values, [((r, c), (r, c - 1)) for r, c in every if 0 < c < col_size - hop])

    def send_round(values, hop):
        moves = []
        for c in range(col_size):
            start = place[c * chips // col_size]
            for a, way in ((0, 1), (1, -1)):
                here = ring[(start + way * (hop - 1)) % chips]
                there = ring[(start + way * hop) % chips]
                moves.append(((2 * here + a, c), (2 * there + a, c)))
        return send(values, moves)

    def swap_cores(values):
        return send(values, [((r, c), (r ^ 1, c)) for r, c in every])

    distance = np.zeros((row_size, col_size), np.int32)
    for r, c in every:
        gap = place[r // 2] - place[c * chips // col_size]
        distance[r, c] = (gap if r % 2 == 0 else -gap) % chips
    my_distance = jnp.asarray(distance)[row_index, col_index].reshape(1)

    sets = line_sets(col_size)
    owners = np.array(
        [[z] + [owner(z, sets[j][z]) for j in range(col_size - 1)] for z in range(col_size)], np.int32
    )
    my_owners = jnp.asarray(owners)[col_index]

    parts = whiten_parts(spectra, quality)
    arrivals = {("dn", h): [] for h in range(col_size - 1)} | {("up", h): [] for h in range(col_size - 1)}
    for p in range(PARTS):
        down, up = parts[p], parts[p]
        for hop in range(col_size - 1):
            down, up = send_down(down, hop), send_up(up, hop)
            arrivals[("dn", hop)].append(down)
            arrivals[("up", hop)].append(up)

    rows_sets, cols_sets = [], []
    for j in range(col_size):
        if j == 0:
            mine = list(parts)
        else:
            kinds = sorted(set(sets[j - 1]))
            choice = jnp.asarray(np.array([kinds.index(k) for k in sets[j - 1]], np.int32))[col_index].reshape(1)
            mine = [pick(choice, [arrivals[k][p] for k in kinds]) for p in range(PARTS)]
        near, far = [], []
        for p in range(PARTS):
            held = [mine[p]]
            for hop in range(1, chips):
                held.append(send_round(held[-1], hop))
            near.append(pick(my_distance, held))
            far.append(swap_cores(near[-1]))
        rows_sets.append(mine)
        cols_sets.append([near, far])

    row_count = channels * col_size
    col_count = row_count * row_size // col_size
    half_cols = col_count // 2
    norm_scale = 1.0 / math.sqrt(spectra.shape[2] // 2 * bins)
    local_mask = lax.dynamic_slice(
        tile_mask,
        (row_index * (row_count // BLK), col_index * (col_count // BLK)),
        (row_count // BLK, col_count // BLK),
    ).astype(jnp.float32)
    matrices = lag_matrices(bins)
    out_shape = (LAGS, row_count, col_count)
    out = None
    for t in range(col_size):
        units = tuple((t, b) for b in range(t + 1)) + tuple((a, t) for a in range(t))
        row_owner = my_owners[np.array([a for a, _ in units])]
        col_owner = my_owners[np.array([b for _, b in units])]
        near_at = core * half_cols + col_owner * channels
        far_at = (1 - core) * half_cols + col_owner * channels
        offsets = jnp.stack([row_owner * channels, near_at, far_at]).astype(jnp.int32)
        scales = jnp.stack(
            [local_mask[row_owner, near_at // BLK], local_mask[row_owner, far_at // BLK]]
        ) * norm_scale
        out = correlate(units, offsets, scales, rows_sets, cols_sets, matrices, out, out_shape)
    return out


def solution(mesh):
    def per_device(spectra, quality, tile_mask):
        even = mesh.shape["row"] == 2 * mesh.shape["col"]
        plan = line_plan if even and spectra.shape[1] == BLK else general_plan
        return plan(mesh, spectra, quality, tile_mask)

    placed = (P(None, AXES, None), P(AXES), P())
    return jax.shard_map(
        per_device, mesh=mesh, in_specs=placed, out_specs=P(None, "row", "col"), check_vma=False
    )
```

```python
import functools
import math

import jax
import jax.numpy as jnp
import numpy as np
from jax import lax
from jax.experimental import pallas as pl
from jax.experimental.pallas import tpu as pltpu
from jax.sharding import PartitionSpec as P

BLK = 128
LAGS = 64
PARTS = 4
STEP_BINS = 8
GROUP = 8
VMEM_BYTES = 58 * 1024 * 1024
AXES = ("row", "col")
DEPTH = 3
LIGHT = pl.CostEstimate(flops=0, bytes_accessed=1024, transcendentals=0)
TOKEN = jax.ShapeDtypeStruct((8, 128), jnp.int32)


def whiten(spectra, quality):
    values = spectra.astype(jnp.float32)
    half_width = values.shape[2] // 2
    real_part = values[:, :, :half_width]
    imag_part = values[:, :, half_width:]
    energy = real_part * real_part + imag_part * imag_part
    mean_energy = jnp.mean(energy, axis=0, keepdims=True)
    factor = quality.astype(jnp.float32)[None, :, None] / jnp.sqrt(energy + mean_energy + 1e-06)
    return jnp.concatenate([real_part * factor, imag_part * factor], axis=2).astype(jnp.bfloat16)


def lag_angles(bins):
    lag_offset = np.arange(LAGS, dtype=np.float32) - np.float32(LAGS / 2)
    frequency = np.arange(bins, dtype=np.float32) + np.float32(1.0)
    scaled = np.float32(2.0 * math.pi) * frequency[None, :]
    return (scaled * lag_offset[:, None]) / np.float32(2.0 * LAGS)


def general_plan(mesh, spectra, quality, tile_mask):
    bins, _, width = spectra.shape
    row_size, col_size = mesh.shape["row"], mesh.shape["col"]
    white = whiten(spectra, quality)
    row_block = lax.all_gather(white, "col", axis=1, tiled=True)
    row_index, col_index = lax.axis_index("row"), lax.axis_index("col")
    row_count = row_block.shape[1]
    col_count = row_count * row_size // col_size
    share_of = row_size // col_size
    zeros = jnp.zeros_like(row_block)
    sectioned = jnp.concatenate(
        [jnp.where(row_index == share_of * col_index + s, row_block, zeros) for s in range(share_of)], axis=1
    )
    share = lax.psum_scatter(sectioned, "row", scatter_dimension=1, tiled=True)
    col_block = lax.all_gather(share, "row", axis=1, tiled=True)
    half_width = width // 2
    turned = jnp.concatenate([-col_block[:, :, half_width:], col_block[:, :, :half_width]], axis=2)
    both_parts = jnp.concatenate([col_block, turned], axis=1)
    angles = lag_angles(bins)
    basis = jnp.asarray(np.stack([np.cos(angles), -np.sin(angles)], axis=1)).astype(jnp.bfloat16)
    mask = jnp.repeat(jnp.repeat(tile_mask.astype(jnp.float32), BLK, axis=0), BLK, axis=1)
    local_mask = lax.dynamic_slice(mask, (row_index * row_count, col_index * col_count), (row_count, col_count))
    norm_scale = 1.0 / math.sqrt(half_width * bins)
    step = math.gcd(row_count, BLK)

    def fill(index, result):
        rows_here = lax.dynamic_slice_in_dim(row_block, index * step, step, 1)
        cross = jnp.einsum("fiw,fjw->fij", rows_here, both_parts, preferred_element_type=jnp.float32)
        cross = cross.astype(jnp.bfloat16).reshape(bins, step, 2, col_count)
        lagged = jnp.einsum("lpf,fipj->lij", basis, cross, preferred_element_type=jnp.float32)
        mask_rows = lax.dynamic_slice_in_dim(local_mask, index * step, step, 0)
        piece = (lagged * norm_scale * mask_rows[None]).astype(jnp.bfloat16)
        return lax.dynamic_update_slice_in_dim(result, piece, index * step, 1)

    initial = jnp.zeros((LAGS, row_count, col_count), jnp.bfloat16)
    return lax.fori_loop(0, row_count // step, fill, initial)


def whiten_kernel(spectra_ref, quality_ref, *out_refs):
    bins, _, width = spectra_ref.shape
    half_width = width // 2
    total = jnp.zeros((spectra_ref.shape[1], half_width), jnp.float32)
    for f in range(bins):
        real_part = spectra_ref[f, :, :half_width].astype(jnp.float32)
        imag_part = spectra_ref[f, :, half_width:].astype(jnp.float32)
        total = total + (real_part * real_part + imag_part * imag_part)
    offset = total * (1.0 / bins) + 1e-06
    quality = quality_ref[...].astype(jnp.float32)
    for f in range(bins):
        real_part = spectra_ref[f, :, :half_width].astype(jnp.float32)
        imag_part = spectra_ref[f, :, half_width:].astype(jnp.float32)
        factor = quality * lax.rsqrt(real_part * real_part + imag_part * imag_part + offset)
        white_real = (real_part * factor).astype(jnp.bfloat16)
        white_imag = (imag_part * factor).astype(jnp.bfloat16)
        first = 0
        for out_ref in out_refs:
            size = out_ref.shape[0]
            if first <= f % bins < first + size:
                out_ref[f - first, :, :half_width] = white_real
                out_ref[f - first, :, half_width:] = white_imag
            first = (first + size) % bins


def whiten_parts(spectra, quality, sizes):
    bins, channels, width = spectra.shape
    rows = 16
    return pl.pallas_call(
        whiten_kernel,
        grid=(channels // rows,),
        in_specs=[
            pl.BlockSpec((bins, rows, width), lambda i: (0, i, 0)),
            pl.BlockSpec((rows, 1), lambda i: (i, 0)),
        ],
        out_specs=[pl.BlockSpec((size, rows, width), lambda i: (0, i, 0)) for size in sizes],
        out_shape=[jax.ShapeDtypeStruct((size, channels, width), jnp.bfloat16) for size in sizes],
        compiler_params=pltpu.CompilerParams(vmem_limit_bytes=VMEM_BYTES),
        name="whiten",
    )(spectra, quality[:, None])


def pick_kernel(starts, choice_ref, *refs):
    sources, (target_ref, buffer, in_sem, out_sem) = refs[: len(starts)], refs[-4:]
    pieces = in_sem.shape[0]
    block = target_ref.shape[0] // pieces

    def copy_in(index, piece):
        return pltpu.make_async_copy(
            sources[index].at[pl.ds(starts[index] + piece * block, block)],
            buffer.at[pl.ds(piece * block, block)],
            in_sem.at[piece],
        )

    def copy_out(piece):
        here = pl.ds(piece * block, block)
        return pltpu.make_async_copy(buffer.at[here], target_ref.at[here], out_sem.at[piece])

    for index in range(len(starts)):

        @pl.when(choice_ref[0] == index)
        def _():
            for piece in range(pieces):
                copy_in(index, piece).start()

    for piece in range(pieces):
        copy_in(0, piece).wait()
        copy_out(piece).start()
    for piece in range(pieces):
        copy_out(piece).wait()


def pick(choice, sources, starts, size, *after):
    shape = (size,) + sources[0].shape[1:]
    pieces = min(4, size)
    any_spec = pl.BlockSpec(memory_space=pl.ANY)
    return pl.pallas_call(
        functools.partial(pick_kernel, tuple(starts)),
        grid_spec=pltpu.PrefetchScalarGridSpec(
            num_scalar_prefetch=1,
            grid=(1,),
            in_specs=[any_spec] * (len(sources) + len(after)),
            out_specs=any_spec,
            scratch_shapes=[
                pltpu.VMEM(shape, jnp.bfloat16),
                pltpu.SemaphoreType.DMA((pieces,)),
                pltpu.SemaphoreType.DMA((pieces,)),
            ],
        ),
        out_shape=jax.ShapeDtypeStruct(shape, jnp.bfloat16),
        cost_estimate=LIGHT,
        compiler_params=pltpu.CompilerParams(vmem_limit_bytes=VMEM_BYTES),
        name="pick",
    )(choice, *sources, *after)


def hold(value, *after):
    any_spec = pl.BlockSpec(memory_space=pl.ANY)
    return pl.pallas_call(
        lambda *refs: None,
        in_specs=[any_spec] * (1 + len(after)),
        out_specs=any_spec,
        out_shape=jax.ShapeDtypeStruct(value.shape, value.dtype),
        input_output_aliases={0: 0},
        cost_estimate=LIGHT,
        compiler_params=pltpu.CompilerParams(vmem_limit_bytes=VMEM_BYTES),
        name="hold",
    )(value, *after)


def correlate_kernel(row_sets, col_sets, x_from, y_from, offset_ref, scale_ref, *refs):
    n_rows, n_cols, parts = len(x_from), len(y_from), len(x_from[0])
    rest = refs[1 + max(index for one in y_from for half in one for index, _ in half) :]
    even_ref, odd_ref = rest[:2]
    out_ref, _, x_buf, y_buf, cross, out_buf, in_sem, out_sem = rest[-8:]
    per, rows, width = x_buf.shape[1:]
    half_width = width // 2
    groups = rows // GROUP
    cols = 2 * rows
    half = out_buf.shape[1] // 2
    units = n_rows * n_cols
    steps = units * parts
    x_stays, y_stays = n_rows == 1, n_cols == 1

    def source(where):
        index, start = where
        return refs[index].at[pl.ds(start, per)]

    def x_copy(s, c, slot, step):
        return [pltpu.make_async_copy(source(x_from[s][c]), x_buf.at[slot], in_sem.at[lax.rem(step, DEPTH), 0])]

    def y_copies(s, c, slot, step):
        return [
            pltpu.make_async_copy(
                source(y_from[s][h][c]), y_buf.at[slot, :, pl.ds(h * rows, rows)], in_sem.at[lax.rem(step, DEPTH), 1 + h]
            )
            for h in range(2)
        ]

    def slot_of(stays, step):
        return lax.rem(step, parts) if stays else lax.rem(step, DEPTH)

    def fetch(step):
        for s in range(steps):
            unit, c = s // parts, s % parts

            @pl.when(step == s)
            def _():
                if unit == 0 or not x_stays:
                    for copy in x_copy(0 if x_stays else unit, c, slot_of(x_stays, step), step):
                        copy.start()
                if unit == 0 or not y_stays:
                    for copy in y_copies(0 if y_stays else unit, c, slot_of(y_stays, step), step):
                        copy.start()

    def arrive(step):
        def x_wait():
            for copy in x_copy(0, 0, 0, step):
                copy.wait()

        def y_wait():
            for copy in y_copies(0, 0, 0, step):
                copy.wait()

        if x_stays:
            pl.when(step < parts)(x_wait)
        else:
            x_wait()
        if y_stays:
            pl.when(step < parts)(y_wait)
        else:
            y_wait()

    def sets_of(unit):
        return row_sets[0] + (0 if x_stays else unit), col_sets[0] + (0 if y_stays else unit)

    def copies_out(unit, slot):
        row_set, col_set = sets_of(unit)
        row = pl.multiple_of(offset_ref[0, row_set], rows)
        return [
            pltpu.make_async_copy(
                out_buf.at[slot, :, :, pl.ds(h * rows, rows)],
                out_ref.at[:, pl.ds(row, rows), pl.ds(pl.multiple_of(offset_ref[1 + h, col_set], rows), rows)],
                out_sem.at[slot, h],
            )
            for h in range(2)
        ]

    for step in range(min(DEPTH - 1, steps)):
        fetch(jnp.int32(step))

    @pl.loop(0, steps)
    def _(step):
        unit = step // parts
        part = lax.rem(step, parts)
        x_slot, y_slot = slot_of(x_stays, step), slot_of(y_stays, step)

        @pl.when(step + (DEPTH - 1) < steps)
        def _():
            fetch(step + (DEPTH - 1))

        arrive(step)

        @pl.loop(0, per // 2, unroll=True)
        def _(pair):
            results = []
            for f in range(2):
                x = x_buf[x_slot, 2 * pair + f]
                y = y_buf[y_slot, 2 * pair + f]
                turned = jnp.concatenate([x[:, half_width:], -x[:, :half_width]], axis=1)
                stacked = jnp.concatenate([x, turned], axis=0)
                product = lax.dot_general(stacked, y, (((1,), (1,)), ((), ())), preferred_element_type=jnp.float32)
                results.append(product.reshape(2 * groups, GROUP, cols))
            both = jnp.concatenate(results, axis=1).astype(jnp.bfloat16)
            at = pl.multiple_of((part * (per // 2) + pair) * 2 * GROUP, 2 * GROUP)
            cross[:, pl.ds(at, 2 * GROUP), :] = both

        @pl.when(part == parts - 1)
        def _():
            out_slot = lax.rem(unit, 2)

            @pl.when(unit >= 2)
            def _():
                for copy in copies_out(unit - 2, out_slot):
                    copy.wait()

            row_set, col_set = sets_of(unit)
            scale = jnp.concatenate(
                [jnp.full((1, 1, rows), scale_ref[row_set, 2 * col_set + h], jnp.float32) for h in range(2)], axis=2
            )

            @pl.loop(0, groups // 2, unroll=True)
            def _(two):
                evens, odds = [], []
                for g in range(2):
                    even = jnp.dot(even_ref[...], cross[2 * two + g], preferred_element_type=jnp.float32)
                    odd = jnp.dot(odd_ref[...], cross[groups + 2 * two + g], preferred_element_type=jnp.float32)
                    evens.append(even.reshape(half + 1, GROUP, cols))
                    odds.append(odd.reshape(half, GROUP, cols))
                even = jnp.concatenate(evens, axis=1) * scale
                odd = jnp.concatenate(odds, axis=1) * scale
                here = pl.ds(pl.multiple_of(two * 2 * GROUP, 2 * GROUP), 2 * GROUP)
                out_buf[out_slot, half, here, :] = even[0].astype(jnp.bfloat16)
                out_buf[out_slot, 0, here, :] = (even[half] + odd[0]).astype(jnp.bfloat16)
                for d in range(1, half):
                    out_buf[out_slot, half + d, here, :] = (even[d] - odd[d]).astype(jnp.bfloat16)
                    out_buf[out_slot, half - d, here, :] = (even[d] + odd[d]).astype(jnp.bfloat16)

            for copy in copies_out(unit, out_slot):
                copy.start()

    for unit in range(max(0, units - 2), units):
        for copy in copies_out(unit, unit % 2):
            copy.wait()


def correlate(row_sets, col_sets, offsets, scales, rows_of, cols_of, matrices, out, out_shape, after):
    operands = []

    def spread(arrays):
        where = []
        for array in arrays:
            where += [(len(operands), start) for start in range(0, array.shape[0], STEP_BINS)]
            operands.append(array)
        return tuple(where)

    x_from = tuple(spread(rows_of[s]) for s in row_sets)
    y_from = tuple(tuple(spread(half) for half in cols_of[s]) for s in col_sets)
    parts, per = len(x_from[0]), STEP_BINS
    _, rows, width = operands[0].shape
    bins = per * parts
    before = [] if out is None else [out]
    units = len(row_sets) * len(col_sets)
    any_spec = pl.BlockSpec(memory_space=pl.ANY)
    vmem_spec = pl.BlockSpec(memory_space=pltpu.VMEM)
    n_ops = len(operands)
    x_slots = parts if len(row_sets) == 1 else DEPTH
    y_slots = parts if len(col_sets) == 1 else DEPTH
    return pl.pallas_call(
        functools.partial(correlate_kernel, row_sets, col_sets, x_from, y_from),
        grid_spec=pltpu.PrefetchScalarGridSpec(
            num_scalar_prefetch=2,
            grid=(1,),
            in_specs=[any_spec] * n_ops + [vmem_spec] * 2 + [any_spec] * (len(before) + 1),
            out_specs=[any_spec, any_spec],
            scratch_shapes=[
                pltpu.VMEM((x_slots, per, rows, width), jnp.bfloat16),
                pltpu.VMEM((y_slots, per, 2 * rows, width), jnp.bfloat16),
                pltpu.VMEM((2 * rows // GROUP, bins * GROUP, 2 * rows), jnp.bfloat16),
                pltpu.VMEM((2, LAGS, rows, 2 * rows), jnp.bfloat16),
                pltpu.SemaphoreType.DMA((DEPTH, 3)),
                pltpu.SemaphoreType.DMA((2, 2)),
            ],
        ),
        out_shape=[jax.ShapeDtypeStruct(out_shape, jnp.bfloat16), TOKEN],
        input_output_aliases={2 + n_ops + 2: 0} if before else {},
        cost_estimate=LIGHT,
        compiler_params=pltpu.CompilerParams(vmem_limit_bytes=VMEM_BYTES),
        name="correlate",
    )(offsets, scales, *operands, *matrices, *before, after)


def lag_matrices(bins):
    half = LAGS // 2
    angles = lag_angles(bins)[half:]
    last = -lag_angles(bins)[0]
    cosine = np.concatenate([np.cos(angles), np.cos(last)[None]], axis=0)
    sine = np.concatenate([np.sin(last)[None], np.sin(angles)[1:]], axis=0)

    def spread(table):
        table = table.astype(jnp.bfloat16).astype(np.float32)
        return jnp.asarray(np.kron(table, np.eye(GROUP, dtype=np.float32)).astype(jnp.bfloat16))

    return spread(cosine), spread(sine)


def line_plan(mesh, spectra, quality, tile_mask):
    row_size, col_size = mesh.shape["row"], mesh.shape["col"]
    chips = row_size // 2
    bins, channels, _ = spectra.shape
    row_index, col_index = lax.axis_index("row"), lax.axis_index("col")
    core = row_index % 2
    ring = [i ^ (i >> 1) for i in range(chips)]
    place = [ring.index(k) for k in range(chips)]
    every = [(r, c) for r in range(row_size) for c in range(col_size)]

    def send(values, moves):
        pairs = [(r * col_size + c, s * col_size + d) for (r, c), (s, d) in moves]
        return lax.ppermute(values, AXES, pairs)

    def along(values, line):
        return send(values, [((r, c), (r, d)) for r in range(row_size) for c, d in line])

    def send_round(values, hop):
        moves = []
        for c in range(col_size):
            for a, way in ((0, 1), (1, -1)):
                here = ring[(place[c] + way * (hop - 1)) % chips]
                there = ring[(place[c] + way * hop) % chips]
                moves.append(((2 * here + a, c), (2 * there + a, c)))
        return send(values, moves)

    def swap_cores(values):
        return send(values, [((r, c), (r ^ 1, c)) for r, c in every])

    outer, inner, out_pass = [(0, 1), (1, 0), (2, 3), (3, 2)], [(1, 2), (2, 1)], [(1, 0), (2, 3)]
    owners = np.array([[0, 1, 2, 3], [1, 0, 2, 3], [2, 3, 1, 0], [3, 2, 1, 0]], np.int32)

    distance = np.zeros((row_size, col_size), np.int32)
    for r, c in every:
        gap = place[r // 2] - place[c]
        distance[r, c] = (gap if r % 2 == 0 else -gap) % chips
    my_distance = jnp.asarray(distance)[row_index, col_index].reshape(1)
    my_owners = jnp.asarray(owners)[col_index]
    at_end = ((col_index == 0) | (col_index == col_size - 1)).astype(jnp.int32).reshape(1)

    n_parts = PARTS
    short = bins // n_parts
    white, *own = whiten_parts(spectra, quality, [bins] + [short] * n_parts)
    row_count = channels * col_size
    col_count = row_count * row_size // col_size
    half_cols = col_count // 2
    norm_scale = 1.0 / math.sqrt(spectra.shape[2] // 2 * bins)
    local_mask = lax.dynamic_slice(
        tile_mask,
        (row_index * (row_count // BLK), col_index * (col_count // BLK)),
        (row_count // BLK, col_count // BLK),
    ).astype(jnp.float32)
    matrices = lag_matrices(bins)
    out_shape = (LAGS, row_count, col_count)
    near_at = core * half_cols + my_owners * channels
    far_at = (1 - core) * half_cols + my_owners * channels
    offsets = jnp.stack([my_owners * channels, near_at, far_at]).astype(jnp.int32)
    tiles = jnp.stack([near_at, far_at], axis=1).reshape(-1) // BLK
    scales = norm_scale * jnp.take(jnp.take(local_mask, my_owners, axis=0), tiles, axis=1)

    rows_of = [list(own)] + [[None] * n_parts for _ in range(1, col_size)]
    near_of = [[None] * n_parts for _ in range(col_size)]
    far_of = [[None] * n_parts for _ in range(col_size)]
    cols_of = [[near_of[j], far_of[j]] for j in range(col_size)]
    out, last = None, own[0]

    def part_of(whole, p):
        return lax.slice_in_dim(whole, p * short, (p + 1) * short, axis=0)

    def take_rows(j, p):
        nonlocal last
        start = p * short
        if j == 2:
            last = pick(at_end, [second_in, second_out], [start, start], short, last)
        else:
            last = pick(at_end, [third_in, third_out[p]], [start, 0], short, last)
            if p + 2 < n_parts:
                third_out[p + 2] = along(part_of(lax.optimization_barrier((third_in, last))[0], p + 2), out_pass)
        rows_of[j][p] = last

    def go_round(j, p):
        nonlocal last
        held = [rows_of[j][p]]
        for hop in range(1, chips):
            held.append(send_round(held[-1], hop))
        last = near_of[j][p] = pick(my_distance, held, [0] * chips, short, last)

    def swap(j):
        for p in range(n_parts):
            far_of[j][p] = swap_cores(near_of[j][p])

    def take_cols(j, p):
        go_round(j, p)
        far_of[j][p] = swap_cores(near_of[j][p])

    def pairs_of(row_sets, col_sets):
        nonlocal out, last
        out, last = correlate(row_sets, col_sets, offsets, scales, rows_of, cols_of, matrices, out, out_shape, last)

    def meet(*values):
        nonlocal last
        values = lax.optimization_barrier((*values, last))
        last = values[-1]
        return values[:-1]

    first, second_in = along(white, outer), along(white, inner)
    for p in range(n_parts):
        go_round(0, p)
    first, second_in, *near_of[0][:] = meet(first, second_in, *near_of[0])

    second_out, third_in = along(second_in, out_pass), along(first, inner)
    swap(0)
    rows_of[1][:] = [part_of(first, p) for p in range(n_parts)]
    pairs_of((1,), (0,))
    pairs_of((0,), (0,))
    for p in range(n_parts):
        go_round(1, p)
    second_in, second_out, third_in, out, *near_of[1][:] = meet(second_in, second_out, third_in, out, *near_of[1])

    third_out = [along(part_of(third_in, p), out_pass) for p in range(2)] + [None] * (n_parts - 2)
    swap(1)
    for p in range(n_parts):
        take_rows(2, p)
    pairs_of((0, 1), (1,))
    take_rows(3, 0)
    pairs_of((2,), (0, 1))
    take_rows(3, 1)
    take_cols(2, 0)
    take_cols(2, 1)
    take_rows(3, 2)
    take_cols(2, 2)
    take_cols(2, 3)
    take_cols(3, 0)
    take_rows(3, 3)
    take_cols(3, 1)
    pairs_of((0, 1, 2), (2,))
    take_cols(3, 2)
    pairs_of((3,), (0, 1, 2))
    take_cols(3, 3)
    pairs_of((0, 1, 2, 3), (3,))
    return out


def solution(mesh):
    def per_device(spectra, quality, tile_mask):
        row_size, col_size = mesh.shape["row"], mesh.shape["col"]
        fits = col_size == 4 and row_size == 2 * col_size and spectra.shape[1] == BLK
        fits = fits and spectra.shape[0] % (PARTS * STEP_BINS) == 0
        plan = line_plan if fits else general_plan
        return plan(mesh, spectra, quality, tile_mask)

    placed = (P(None, AXES, None), P(AXES), P())
    return jax.shard_map(
        per_device, mesh=mesh, in_specs=placed, out_specs=P(None, "row", "col"), check_vma=False
    )
```

```python
import functools
import math

import jax
import jax.numpy as jnp
import numpy as np
from jax import lax
from jax.experimental import pallas as pl
from jax.experimental.pallas import tpu as pltpu
from jax.sharding import PartitionSpec as P

BLK = 128
LAGS = 64
PARTS = 4
STEP_BINS = 8
GROUP = 8
VMEM_BYTES = 58 * 1024 * 1024
AXES = ("row", "col")
DEPTH = 5
LIGHT = pl.CostEstimate(flops=0, bytes_accessed=1024, transcendentals=0)
TOKEN = jax.ShapeDtypeStruct((8, 128), jnp.int32)


def whiten(spectra, quality):
    values = spectra.astype(jnp.float32)
    half_width = values.shape[2] // 2
    real_part = values[:, :, :half_width]
    imag_part = values[:, :, half_width:]
    energy = real_part * real_part + imag_part * imag_part
    mean_energy = jnp.mean(energy, axis=0, keepdims=True)
    factor = quality.astype(jnp.float32)[None, :, None] / jnp.sqrt(energy + mean_energy + 1e-06)
    return jnp.concatenate([real_part * factor, imag_part * factor], axis=2).astype(jnp.bfloat16)


def lag_angles(bins):
    lag_offset = np.arange(LAGS, dtype=np.float32) - np.float32(LAGS / 2)
    frequency = np.arange(bins, dtype=np.float32) + np.float32(1.0)
    scaled = np.float32(2.0 * math.pi) * frequency[None, :]
    return (scaled * lag_offset[:, None]) / np.float32(2.0 * LAGS)


def general_plan(mesh, spectra, quality, tile_mask):
    bins, _, width = spectra.shape
    row_size, col_size = mesh.shape["row"], mesh.shape["col"]
    white = whiten(spectra, quality)
    row_block = lax.all_gather(white, "col", axis=1, tiled=True)
    row_index, col_index = lax.axis_index("row"), lax.axis_index("col")
    row_count = row_block.shape[1]
    col_count = row_count * row_size // col_size
    share_of = row_size // col_size
    zeros = jnp.zeros_like(row_block)
    sectioned = jnp.concatenate(
        [jnp.where(row_index == share_of * col_index + s, row_block, zeros) for s in range(share_of)], axis=1
    )
    share = lax.psum_scatter(sectioned, "row", scatter_dimension=1, tiled=True)
    col_block = lax.all_gather(share, "row", axis=1, tiled=True)
    half_width = width // 2
    turned = jnp.concatenate([-col_block[:, :, half_width:], col_block[:, :, :half_width]], axis=2)
    both_parts = jnp.concatenate([col_block, turned], axis=1)
    angles = lag_angles(bins)
    basis = jnp.asarray(np.stack([np.cos(angles), -np.sin(angles)], axis=1)).astype(jnp.bfloat16)
    mask = jnp.repeat(jnp.repeat(tile_mask.astype(jnp.float32), BLK, axis=0), BLK, axis=1)
    local_mask = lax.dynamic_slice(mask, (row_index * row_count, col_index * col_count), (row_count, col_count))
    norm_scale = 1.0 / math.sqrt(half_width * bins)
    step = math.gcd(row_count, BLK)

    def fill(index, result):
        rows_here = lax.dynamic_slice_in_dim(row_block, index * step, step, 1)
        cross = jnp.einsum("fiw,fjw->fij", rows_here, both_parts, preferred_element_type=jnp.float32)
        cross = cross.astype(jnp.bfloat16).reshape(bins, step, 2, col_count)
        lagged = jnp.einsum("lpf,fipj->lij", basis, cross, preferred_element_type=jnp.float32)
        mask_rows = lax.dynamic_slice_in_dim(local_mask, index * step, step, 0)
        piece = (lagged * norm_scale * mask_rows[None]).astype(jnp.bfloat16)
        return lax.dynamic_update_slice_in_dim(result, piece, index * step, 1)

    initial = jnp.zeros((LAGS, row_count, col_count), jnp.bfloat16)
    return lax.fori_loop(0, row_count // step, fill, initial)


def whiten_kernel(spectra_ref, quality_ref, *out_refs):
    bins, _, width = spectra_ref.shape
    half_width = width // 2
    total = jnp.zeros((spectra_ref.shape[1], half_width), jnp.float32)
    for f in range(bins):
        real_part = spectra_ref[f, :, :half_width].astype(jnp.float32)
        imag_part = spectra_ref[f, :, half_width:].astype(jnp.float32)
        total = total + (real_part * real_part + imag_part * imag_part)
    offset = total * (1.0 / bins) + 1e-06
    quality = quality_ref[...].astype(jnp.float32)
    for f in range(bins):
        real_part = spectra_ref[f, :, :half_width].astype(jnp.float32)
        imag_part = spectra_ref[f, :, half_width:].astype(jnp.float32)
        factor = quality * lax.rsqrt(real_part * real_part + imag_part * imag_part + offset)
        white_real = (real_part * factor).astype(jnp.bfloat16)
        white_imag = (imag_part * factor).astype(jnp.bfloat16)
        first = 0
        for out_ref in out_refs:
            size = out_ref.shape[0]
            if first <= f % bins < first + size:
                out_ref[f - first, :, :half_width] = white_real
                out_ref[f - first, :, half_width:] = white_imag
            first = (first + size) % bins


def whiten_parts(spectra, quality, sizes):
    bins, channels, width = spectra.shape
    rows = 16
    return pl.pallas_call(
        whiten_kernel,
        grid=(channels // rows,),
        in_specs=[
            pl.BlockSpec((bins, rows, width), lambda i: (0, i, 0)),
            pl.BlockSpec((rows, 1), lambda i: (i, 0)),
        ],
        out_specs=[pl.BlockSpec((size, rows, width), lambda i: (0, i, 0)) for size in sizes],
        out_shape=[jax.ShapeDtypeStruct((size, channels, width), jnp.bfloat16) for size in sizes],
        compiler_params=pltpu.CompilerParams(vmem_limit_bytes=VMEM_BYTES),
        name="whiten",
    )(spectra, quality[:, None])


def pick_kernel(starts, choice_ref, *refs):
    sources, (target_ref, buffer, in_sem, out_sem) = refs[: len(starts)], refs[-4:]
    pieces = in_sem.shape[0]
    block = target_ref.shape[0] // pieces

    def copy_in(index, piece):
        return pltpu.make_async_copy(
            sources[index].at[pl.ds(starts[index] + piece * block, block)],
            buffer.at[pl.ds(piece * block, block)],
            in_sem.at[piece],
        )

    def copy_out(piece):
        here = pl.ds(piece * block, block)
        return pltpu.make_async_copy(buffer.at[here], target_ref.at[here], out_sem.at[piece])

    for index in range(len(starts)):

        @pl.when(choice_ref[0] == index)
        def _():
            for piece in range(pieces):
                copy_in(index, piece).start()

    for piece in range(pieces):
        copy_in(0, piece).wait()
        copy_out(piece).start()
    for piece in range(pieces):
        copy_out(piece).wait()


def pick(choice, sources, starts, size, *after):
    shape = (size,) + sources[0].shape[1:]
    pieces = min(4, size)
    any_spec = pl.BlockSpec(memory_space=pl.ANY)
    return pl.pallas_call(
        functools.partial(pick_kernel, tuple(starts)),
        grid_spec=pltpu.PrefetchScalarGridSpec(
            num_scalar_prefetch=1,
            grid=(1,),
            in_specs=[any_spec] * (len(sources) + len(after)),
            out_specs=any_spec,
            scratch_shapes=[
                pltpu.VMEM(shape, jnp.bfloat16),
                pltpu.SemaphoreType.DMA((pieces,)),
                pltpu.SemaphoreType.DMA((pieces,)),
            ],
        ),
        out_shape=jax.ShapeDtypeStruct(shape, jnp.bfloat16),
        cost_estimate=LIGHT,
        compiler_params=pltpu.CompilerParams(vmem_limit_bytes=VMEM_BYTES),
        name="pick",
    )(choice, *sources, *after)


def hold(value, *after):
    any_spec = pl.BlockSpec(memory_space=pl.ANY)
    return pl.pallas_call(
        lambda *refs: None,
        in_specs=[any_spec] * (1 + len(after)),
        out_specs=any_spec,
        out_shape=jax.ShapeDtypeStruct(value.shape, value.dtype),
        input_output_aliases={0: 0},
        cost_estimate=LIGHT,
        compiler_params=pltpu.CompilerParams(vmem_limit_bytes=VMEM_BYTES),
        name="hold",
    )(value, *after)


def correlate_kernel(row_sets, col_sets, x_from, y_from, offset_ref, scale_ref, *refs):
    n_rows, n_cols, parts = len(x_from), len(y_from), len(x_from[0])
    rest = refs[1 + max(index for one in y_from for half in one for index, _ in half) :]
    even_ref, odd_ref = rest[:2]
    out_ref, _, x_buf, y_buf, cross, out_buf, in_sem, out_sem = rest[-8:]
    per, rows, width = x_buf.shape[1:]
    half_width = width // 2
    groups = rows // GROUP
    cols = 2 * rows
    half = out_buf.shape[1] // 2
    units = n_rows * n_cols
    steps = units * parts
    x_stays, y_stays = n_rows == 1, n_cols == 1

    def source(where):
        index, start = where
        return refs[index].at[pl.ds(start, per)]

    def x_copy(s, c, slot, step):
        return [pltpu.make_async_copy(source(x_from[s][c]), x_buf.at[slot], in_sem.at[lax.rem(step, DEPTH), 0])]

    def y_copies(s, c, slot, step):
        return [
            pltpu.make_async_copy(
                source(y_from[s][h][c]), y_buf.at[slot, :, pl.ds(h * rows, rows)], in_sem.at[lax.rem(step, DEPTH), 1 + h]
            )
            for h in range(2)
        ]

    def slot_of(stays, step):
        return lax.rem(step, parts) if stays else lax.rem(step, DEPTH)

    def fetch(step):
        for s in range(steps):
            unit, c = s // parts, s % parts

            @pl.when(step == s)
            def _():
                if unit == 0 or not x_stays:
                    for copy in x_copy(0 if x_stays else unit, c, slot_of(x_stays, step), step):
                        copy.start()
                if unit == 0 or not y_stays:
                    for copy in y_copies(0 if y_stays else unit, c, slot_of(y_stays, step), step):
                        copy.start()

    def arrive(step):
        def x_wait():
            for copy in x_copy(0, 0, 0, step):
                copy.wait()

        def y_wait():
            for copy in y_copies(0, 0, 0, step):
                copy.wait()

        if x_stays:
            pl.when(step < parts)(x_wait)
        else:
            x_wait()
        if y_stays:
            pl.when(step < parts)(y_wait)
        else:
            y_wait()

    def sets_of(unit):
        return row_sets[0] + (0 if x_stays else unit), col_sets[0] + (0 if y_stays else unit)

    def copies_out(unit, slot):
        row_set, col_set = sets_of(unit)
        row = pl.multiple_of(offset_ref[0, row_set], rows)
        return [
            pltpu.make_async_copy(
                out_buf.at[slot, :, :, pl.ds(h * rows, rows)],
                out_ref.at[:, pl.ds(row, rows), pl.ds(pl.multiple_of(offset_ref[1 + h, col_set], rows), rows)],
                out_sem.at[slot, h],
            )
            for h in range(2)
        ]

    for step in range(min(DEPTH - 1, steps)):
        fetch(jnp.int32(step))

    @pl.loop(0, steps)
    def _(step):
        unit = step // parts
        part = lax.rem(step, parts)
        x_slot, y_slot = slot_of(x_stays, step), slot_of(y_stays, step)

        @pl.when(step + (DEPTH - 1) < steps)
        def _():
            fetch(step + (DEPTH - 1))

        arrive(step)

        @pl.loop(0, per // 2, unroll=True)
        def _(pair):
            results = []
            for f in range(2):
                x = x_buf[x_slot, 2 * pair + f]
                y = y_buf[y_slot, 2 * pair + f]
                turned = jnp.concatenate([x[:, half_width:], -x[:, :half_width]], axis=1)
                stacked = jnp.concatenate([x, turned], axis=0)
                product = lax.dot_general(stacked, y, (((1,), (1,)), ((), ())), preferred_element_type=jnp.float32)
                results.append(product.reshape(2 * groups, GROUP, cols))
            both = jnp.concatenate(results, axis=1).astype(jnp.bfloat16)
            at = pl.multiple_of((part * (per // 2) + pair) * 2 * GROUP, 2 * GROUP)
            cross[:, pl.ds(at, 2 * GROUP), :] = both

        @pl.when(part == parts - 1)
        def _():
            out_slot = lax.rem(unit, 2)

            @pl.when(unit >= 2)
            def _():
                for copy in copies_out(unit - 2, out_slot):
                    copy.wait()

            row_set, col_set = sets_of(unit)
            scale = jnp.concatenate(
                [jnp.full((1, 1, rows), scale_ref[row_set, 2 * col_set + h], jnp.float32) for h in range(2)], axis=2
            )

            @pl.loop(0, groups // 2, unroll=True)
            def _(two):
                evens, odds = [], []
                for g in range(2):
                    even = jnp.dot(even_ref[...], cross[2 * two + g], preferred_element_type=jnp.float32)
                    odd = jnp.dot(odd_ref[...], cross[groups + 2 * two + g], preferred_element_type=jnp.float32)
                    evens.append(even.reshape(half + 1, GROUP, cols))
                    odds.append(odd.reshape(half, GROUP, cols))
                even = jnp.concatenate(evens, axis=1) * scale
                odd = jnp.concatenate(odds, axis=1) * scale
                here = pl.ds(pl.multiple_of(two * 2 * GROUP, 2 * GROUP), 2 * GROUP)
                out_buf[out_slot, half, here, :] = even[0].astype(jnp.bfloat16)
                out_buf[out_slot, 0, here, :] = (even[half] + odd[0]).astype(jnp.bfloat16)
                for d in range(1, half):
                    out_buf[out_slot, half + d, here, :] = (even[d] - odd[d]).astype(jnp.bfloat16)
                    out_buf[out_slot, half - d, here, :] = (even[d] + odd[d]).astype(jnp.bfloat16)

            for copy in copies_out(unit, out_slot):
                copy.start()

    for unit in range(max(0, units - 2), units):
        for copy in copies_out(unit, unit % 2):
            copy.wait()


def correlate(row_sets, col_sets, offsets, scales, rows_of, cols_of, matrices, out, out_shape, after):
    operands = []

    def spread(arrays):
        where = []
        for array in arrays:
            where += [(len(operands), start) for start in range(0, array.shape[0], STEP_BINS)]
            operands.append(array)
        return tuple(where)

    x_from = tuple(spread(rows_of[s]) for s in row_sets)
    y_from = tuple(tuple(spread(half) for half in cols_of[s]) for s in col_sets)
    parts, per = len(x_from[0]), STEP_BINS
    _, rows, width = operands[0].shape
    bins = per * parts
    before = [] if out is None else [out]
    units = len(row_sets) * len(col_sets)
    any_spec = pl.BlockSpec(memory_space=pl.ANY)
    vmem_spec = pl.BlockSpec(memory_space=pltpu.VMEM)
    n_ops = len(operands)
    x_slots = parts if len(row_sets) == 1 else DEPTH
    y_slots = parts if len(col_sets) == 1 else DEPTH
    return pl.pallas_call(
        functools.partial(correlate_kernel, row_sets, col_sets, x_from, y_from),
        grid_spec=pltpu.PrefetchScalarGridSpec(
            num_scalar_prefetch=2,
            grid=(1,),
            in_specs=[any_spec] * n_ops + [vmem_spec] * 2 + [any_spec] * (len(before) + 1),
            out_specs=[any_spec, any_spec],
            scratch_shapes=[
                pltpu.VMEM((x_slots, per, rows, width), jnp.bfloat16),
                pltpu.VMEM((y_slots, per, 2 * rows, width), jnp.bfloat16),
                pltpu.VMEM((2 * rows // GROUP, bins * GROUP, 2 * rows), jnp.bfloat16),
                pltpu.VMEM((2, LAGS, rows, 2 * rows), jnp.bfloat16),
                pltpu.SemaphoreType.DMA((DEPTH, 3)),
                pltpu.SemaphoreType.DMA((2, 2)),
            ],
        ),
        out_shape=[jax.ShapeDtypeStruct(out_shape, jnp.bfloat16), TOKEN],
        input_output_aliases={2 + n_ops + 2: 0} if before else {},
        cost_estimate=LIGHT,
        compiler_params=pltpu.CompilerParams(vmem_limit_bytes=VMEM_BYTES),
        name="correlate",
    )(offsets, scales, *operands, *matrices, *before, after)


def lag_matrices(bins):
    half = LAGS // 2
    angles = lag_angles(bins)[half:]
    last = -lag_angles(bins)[0]
    cosine = np.concatenate([np.cos(angles), np.cos(last)[None]], axis=0)
    sine = np.concatenate([np.sin(last)[None], np.sin(angles)[1:]], axis=0)

    def spread(table):
        table = table.astype(jnp.bfloat16).astype(np.float32)
        return jnp.asarray(np.kron(table, np.eye(GROUP, dtype=np.float32)).astype(jnp.bfloat16))

    return spread(cosine), spread(sine)


def line_plan(mesh, spectra, quality, tile_mask):
    row_size, col_size = mesh.shape["row"], mesh.shape["col"]
    chips = row_size // 2
    bins, channels, _ = spectra.shape
    row_index, col_index = lax.axis_index("row"), lax.axis_index("col")
    core = row_index % 2
    ring = [i ^ (i >> 1) for i in range(chips)]
    place = [ring.index(k) for k in range(chips)]
    every = [(r, c) for r in range(row_size) for c in range(col_size)]

    def send(values, moves):
        pairs = [(r * col_size + c, s * col_size + d) for (r, c), (s, d) in moves]
        return lax.ppermute(values, AXES, pairs)

    def along(values, line):
        return send(values, [((r, c), (r, d)) for r in range(row_size) for c, d in line])

    def send_round(values, hop):
        moves = []
        for c in range(col_size):
            for a, way in ((0, 1), (1, -1)):
                here = ring[(place[c] + way * (hop - 1)) % chips]
                there = ring[(place[c] + way * hop) % chips]
                moves.append(((2 * here + a, c), (2 * there + a, c)))
        return send(values, moves)

    def swap_cores(values):
        return send(values, [((r, c), (r ^ 1, c)) for r, c in every])

    outer, inner, out_pass = [(0, 1), (1, 0), (2, 3), (3, 2)], [(1, 2), (2, 1)], [(1, 0), (2, 3)]
    owners = np.array([[0, 1, 2, 3], [1, 0, 2, 3], [2, 3, 1, 0], [3, 2, 1, 0]], np.int32)

    distance = np.zeros((row_size, col_size), np.int32)
    for r, c in every:
        gap = place[r // 2] - place[c]
        distance[r, c] = (gap if r % 2 == 0 else -gap) % chips
    my_distance = jnp.asarray(distance)[row_index, col_index].reshape(1)
    my_owners = jnp.asarray(owners)[col_index]
    at_end = ((col_index == 0) | (col_index == col_size - 1)).astype(jnp.int32).reshape(1)

    n_parts = PARTS
    short = bins // n_parts
    white, *own = whiten_parts(spectra, quality, [bins] + [short] * n_parts)
    row_count = channels * col_size
    col_count = row_count * row_size // col_size
    half_cols = col_count // 2
    norm_scale = 1.0 / math.sqrt(spectra.shape[2] // 2 * bins)
    local_mask = lax.dynamic_slice(
        tile_mask,
        (row_index * (row_count // BLK), col_index * (col_count // BLK)),
        (row_count // BLK, col_count // BLK),
    ).astype(jnp.float32)
    matrices = lag_matrices(bins)
    out_shape = (LAGS, row_count, col_count)
    near_at = core * half_cols + my_owners * channels
    far_at = (1 - core) * half_cols + my_owners * channels
    offsets = jnp.stack([my_owners * channels, near_at, far_at]).astype(jnp.int32)
    tiles = jnp.stack([near_at, far_at], axis=1).reshape(-1) // BLK
    scales = norm_scale * jnp.take(jnp.take(local_mask, my_owners, axis=0), tiles, axis=1)

    rows_of = [list(own)] + [[None] * n_parts for _ in range(1, col_size)]
    near_of = [[None] * n_parts for _ in range(col_size)]
    far_of = [[None] * n_parts for _ in range(col_size)]
    cols_of = [[near_of[j], far_of[j]] for j in range(col_size)]
    out, last = None, own[0]

    def part_of(whole, p):
        return lax.slice_in_dim(whole, p * short, (p + 1) * short, axis=0)

    def take_rows(j, p):
        nonlocal last
        start = p * short
        if j == 2:
            last = pick(at_end, [second_in, second_out], [start, start], short, last)
        else:
            last = pick(at_end, [third_in, third_out[p]], [start, 0], short, last)
            if p + 2 < n_parts:
                third_out[p + 2] = along(part_of(lax.optimization_barrier((third_in, last))[0], p + 2), out_pass)
        rows_of[j][p] = last

    def go_round(j, p):
        nonlocal last
        held = [rows_of[j][p]]
        for hop in range(1, chips):
            held.append(send_round(held[-1], hop))
        last = near_of[j][p] = pick(my_distance, held, [0] * chips, short, last)

    def swap(j):
        for p in range(n_parts):
            far_of[j][p] = swap_cores(near_of[j][p])

    def take_cols(j, p):
        go_round(j, p)
        far_of[j][p] = swap_cores(near_of[j][p])

    def pairs_of(row_sets, col_sets):
        nonlocal out, last
        out, last = correlate(row_sets, col_sets, offsets, scales, rows_of, cols_of, matrices, out, out_shape, last)

    def meet(*values):
        nonlocal last
        values = lax.optimization_barrier((*values, last))
        last = values[-1]
        return values[:-1]

    first, second_in = along(white, outer), along(white, inner)
    for p in range(n_parts):
        go_round(0, p)
    first, second_in, *near_of[0][:] = meet(first, second_in, *near_of[0])

    second_out, third_in = along(second_in, out_pass), along(first, inner)
    swap(0)
    rows_of[1][:] = [part_of(first, p) for p in range(n_parts)]
    pairs_of((1,), (0,))
    pairs_of((0,), (0,))
    for p in range(n_parts):
        go_round(1, p)
    second_in, second_out, third_in, out, *near_of[1][:] = meet(second_in, second_out, third_in, out, *near_of[1])

    third_out = [along(part_of(third_in, p), out_pass) for p in range(2)] + [None] * (n_parts - 2)
    swap(1)
    for p in range(n_parts):
        take_rows(2, p)
    pairs_of((0, 1), (1,))
    take_rows(3, 0)
    pairs_of((2,), (0, 1))
    take_rows(3, 1)
    take_cols(2, 0)
    take_cols(2, 1)
    take_rows(3, 2)
    take_cols(2, 2)
    take_cols(2, 3)
    take_cols(3, 0)
    take_rows(3, 3)
    take_cols(3, 1)
    pairs_of((0, 1, 2), (2,))
    take_cols(3, 2)
    pairs_of((3,), (0, 1, 2))
    take_cols(3, 3)
    pairs_of((0, 1, 2, 3), (3,))
    return out


def solution(mesh):
    def per_device(spectra, quality, tile_mask):
        row_size, col_size = mesh.shape["row"], mesh.shape["col"]
        fits = col_size == 4 and row_size == 2 * col_size and spectra.shape[1] == BLK
        fits = fits and spectra.shape[0] % (PARTS * STEP_BINS) == 0
        plan = line_plan if fits else general_plan
        return plan(mesh, spectra, quality, tile_mask)

    placed = (P(None, AXES, None), P(AXES), P())
    return jax.shard_map(
        per_device, mesh=mesh, in_specs=placed, out_specs=P(None, "row", "col"), check_vma=False
    )
```
